128 devices in a mesh: pipe: 16 (over y, x_hi, core), tensor: 8 (over z, x_lo).
Axes of the slice: x: 4 (x_hi: 2, x_lo: 2; x = x_hi * 2 + x_lo), y: 4, z: 4, core: 2. Of those that a mesh axis runs over, the one named last changes fastest.
Arguments:
- forward_input: bfloat16 [16, 512, 4096], P('pipe'), may hold values from -6 to 6
- saved_input: bfloat16 [16, 512, 4096], P('pipe'), may hold values from -6 to 6
- gradient_input: bfloat16 [16, 512, 4096], P('pipe'), may hold values from -6 to 6
- roster: int32 [16, 2], P('pipe'), may hold values from 0 to 1
- sign_bits: int32 [4096], replicated, may hold values from 0 to 1
- gain: float32 [16, 2, 4096], P('pipe'), may hold values from 0.5 to 1.5
- w_query: bfloat16 [16, 2, 4096, 4096], P('pipe', None, None, 'tensor'), may hold values from -0.09375 to 0.09375
- w_key: bfloat16 [16, 2, 4096, 1024], P('pipe', None, None, 'tensor'), may hold values from -0.09375 to 0.09375
- w_value: bfloat16 [16, 2, 4096, 1024], P('pipe', None, None, 'tensor'), may hold values from -0.09375 to 0.09375
- w_out: bfloat16 [16, 2, 4096, 4096], P('pipe', None, 'tensor'), may hold values from -0.09375 to 0.09375
Outputs:
- next_activation: bfloat16 [16, 512, 4096], P('pipe')
- next_gradient: bfloat16 [16, 512, 4096], P('pipe')
The draws below stay inside these ranges and needn't reach their ends.
All inputs are finite; a program needn't handle non-finite values.
Results may differ from the reference program's by a relative error of at most 0.015.
Values may be sent and summed in bfloat16 or wider, within the bound.
A program may use at most 192 MiB of HBM per device.

```python
import math
import jax
import jax.numpy as jnp
from jax import lax

D = 4096
Q_HEADS = 32
KV_HEADS = 8
HD = 128
HB = 128
VIRTUAL = 2
ROWS = 512
N_PIPE = 16
N_TENSOR = 8


def place_ends(array, stream_key, low, top_value):
    shape = array.shape
    spot = [jax.random.randint(jax.random.fold_in(stream_key, axis), (), 0, shape[axis]) for axis in range(len(shape))]
    array = array.at[tuple(spot)].set(low)
    longest = shape.index(max(shape))
    spot[longest] = (spot[longest] + 1) % shape[longest]
    return array.at[tuple(spot)].set(top_value)


def levels(key, dims, split, low, largest):
    loudness = 1.0
    for dim, blocks in split:
        heights = jax.random.uniform(jax.random.fold_in(jax.random.fold_in(key, 6), dim), (blocks,), jnp.float32, low / len(split), largest / len(split))
        loudness = loudness * jnp.repeat(jnp.exp(heights), dims[dim] // blocks).reshape((-1,) + (1,) * (len(dims) - 1 - dim))
    return loudness


def gaussian(key, dims, deviation, bound, pieces=(), kind=jnp.bfloat16):
    factor_of = levels(key, dims, pieces, -0.22, 0.18) if pieces else 1.0
    result = jax.random.normal(key, dims, jnp.float32) * deviation * factor_of
    return jnp.minimum(jnp.maximum(result, -bound), bound).astype(kind)


def setup_inputs(seed: int = 0) -> dict:
    streams_of = jax.random.split(jax.random.key(seed), 11)
    forward_input = gaussian(streams_of[0], (N_PIPE, ROWS, D), 1.0, 6.0, ((0, 16),))
    saved_input = gaussian(streams_of[1], (N_PIPE, ROWS, D), 1.0, 6.0, ((0, 16),))
    gradient_input = gaussian(streams_of[2], (N_PIPE, ROWS, D), 1.0, 6.0, ((0, 16),))
    roster = place_ends(jax.random.randint(streams_of[3], (N_PIPE, 2), 0, VIRTUAL), jax.random.fold_in(streams_of[3], 1), 0, VIRTUAL - 1).astype(jnp.int32)
    sign_bits = place_ends(jax.random.randint(streams_of[4], (D,), 0, 2), jax.random.fold_in(streams_of[4], 1), 0, 1).astype(jnp.int32)
    gain = jnp.clip(0.5 + 1.0 * jax.random.uniform(streams_of[5], (N_PIPE, VIRTUAL, D), jnp.float32) ** levels(streams_of[5], (N_PIPE, VIRTUAL, D), ((0, 16),), -0.2, 0.2), 0.5, 1.5)
    w_query = gaussian(streams_of[6], (N_PIPE, VIRTUAL, D, Q_HEADS * HD), D ** -0.5, 0.09375, ((0, 16), (3, 8)))
    w_key = gaussian(streams_of[7], (N_PIPE, VIRTUAL, D, KV_HEADS * HD), D ** -0.5, 0.09375, ((0, 16), (3, 8)))
    w_value = gaussian(streams_of[8], (N_PIPE, VIRTUAL, D, KV_HEADS * HD), D ** -0.5, 0.09375, ((0, 16), (3, 8)))
    w_out = gaussian(streams_of[9], (N_PIPE, VIRTUAL, Q_HEADS * HD, D), (Q_HEADS * HD) ** -0.5, 0.09375, ((0, 16), (2, 8)))
    return dict(forward_input=forward_input, saved_input=saved_input, gradient_input=gradient_input, roster=roster, sign_bits=sign_bits, gain=gain, w_query=w_query, w_key=w_key, w_value=w_value, w_out=w_out)


eps = 1e-05

def hadamard(order):
    index = jnp.arange(order, dtype=jnp.int32)
    common = index[:, None] & index[None, :]
    parity = jnp.zeros((order, order), jnp.int32)
    for place in range(order.bit_length() - 1):
        parity = parity ^ common >> place & 1
    return (1 - 2 * parity).astype(jnp.float32)

def rotate(values, signs):
    count = values.shape[0]
    blocks = (values * signs).reshape(count, -1, HB)
    turned = jnp.einsum('rbk,kj->rbj', blocks, hadamard(HB), precision=lax.Precision.HIGHEST)
    return (turned / math.sqrt(HB)).reshape(count, -1)

def unrotate(values, signs):
    count = values.shape[0]
    blocks = values.astype(jnp.float32).reshape(count, -1, HB)
    turned = jnp.einsum('rbk,kj->rbj', blocks, hadamard(HB), precision=lax.Precision.HIGHEST)
    return (turned / math.sqrt(HB)).reshape(count, -1) * signs

def heads_part(inputs, gains, query_w, key_w, value_w, out_w):
    rows = inputs.shape[0]
    kv_count = key_w.shape[1] // HD
    q_count = query_w.shape[1] // HD
    group = q_count // kv_count
    scale = lax.rsqrt(lax.optimization_barrier(jnp.mean(inputs * inputs, axis=-1, keepdims=True)) + eps)
    normed = (inputs * scale * gains).astype(jnp.bfloat16)
    query = jnp.dot(normed, query_w, preferred_element_type=jnp.float32).astype(jnp.bfloat16)
    keys = jnp.dot(normed, key_w, preferred_element_type=jnp.float32).astype(jnp.bfloat16)
    values = jnp.dot(normed, value_w, preferred_element_type=jnp.float32).astype(jnp.bfloat16)
    query = query.reshape(rows, kv_count, group, HD).astype(jnp.float32)
    keys = keys.reshape(rows, kv_count, HD).astype(jnp.float32)
    values = values.reshape(rows, kv_count, HD).astype(jnp.float32)
    scores = jnp.einsum('qkgd,skd->kgqs', query, keys) / math.sqrt(HD)
    position = jnp.arange(rows, dtype=jnp.int32)
    allowed = position[:, None] >= position[None, :]
    scores = jnp.where(allowed, scores, -1e+30)
    top = lax.optimization_barrier(jnp.max(scores, axis=-1, keepdims=True))
    expo = jnp.exp(scores - top)
    probs = (expo / lax.optimization_barrier(jnp.sum(expo, axis=-1, keepdims=True))).astype(jnp.bfloat16)
    context = jnp.einsum('kgqs,skd->qkgd', probs.astype(jnp.float32), values).astype(jnp.bfloat16)
    context = context.reshape(rows, q_count * HD)
    return jnp.dot(context, out_w, preferred_element_type=jnp.float32)

def group_weights(query_w, key_w, value_w, out_w, index):
    q_width = query_w.shape[1] // N_TENSOR
    kv_width = key_w.shape[1] // N_TENSOR
    return (query_w[:, index * q_width:(index + 1) * q_width], key_w[:, index * kv_width:(index + 1) * kv_width], value_w[:, index * kv_width:(index + 1) * kv_width], out_w[index * q_width:(index + 1) * q_width, :])

def reference(forward_input, saved_input, gradient_input, roster, sign_bits, gain, w_query, w_key, w_value, w_out):
    signs = (2 * sign_bits - 1).astype(jnp.float32)

    def section(items):
        arrived, stored, incoming, plan, gains, query_w, key_w, value_w, out_w = items
        front = plan[0]
        back = plan[1]
        inputs = unrotate(arrived, signs)
        grad = unrotate(incoming, signs)
        saved = stored.astype(jnp.float32)
        mixed = jnp.zeros_like(inputs)
        pulled = jnp.zeros_like(grad)
        for index in range(N_TENSOR):
            fq, fk, fv, fo = group_weights(query_w[front], key_w[front], value_w[front], out_w[front], index)
            term = heads_part(inputs, gains[front], fq, fk, fv, fo)
            mixed = mixed + term.astype(jnp.bfloat16).astype(jnp.float32)
            bq, bk, bv, bo = group_weights(query_w[back], key_w[back], value_w[back], out_w[back], index)
            gains_back = gains[back]
            _, pull = jax.vjp(lambda v: heads_part(v, gains_back, bq, bk, bv, bo), saved)
            back_term = pull(grad)[0]
            pulled = pulled + back_term.astype(jnp.bfloat16).astype(jnp.float32)
        sent_activation = rotate(inputs + mixed, signs).astype(jnp.bfloat16)
        sent_gradient = rotate(grad + pulled, signs).astype(jnp.bfloat16)
        return (sent_activation, sent_gradient)
    sent_activation, sent_gradient = lax.map(section, (forward_input, saved_input, gradient_input, roster, gain, w_query, w_key, w_value, w_out))
    return (jnp.roll(sent_activation, 1, axis=0), jnp.roll(sent_gradient, -1, axis=0))
```

```python
import functools
import math

import jax
import jax.numpy as jnp
from jax import lax
from jax.experimental import pallas as pl
from jax.experimental.pallas import tpu as pltpu
from jax.sharding import PartitionSpec as P

MESH = pl.DeviceIdType.MESH
D = 4096
ROWS = 512
HD = 128
HB = 128
HEADS = 4
BLOCK = 64
CA = 2304
CB = D - CA
HALF = CB // 2
TILE = 256
EPS = 1e-05
UNIT = 1.0 / math.sqrt(HB)
SM = 1.0 / math.sqrt(HD)
A = pl.ds(0, CA)
B = pl.ds(CA, CB)
BL = pl.ds(CA, HALF)
BR = pl.ds(CA + HALF, HALF)
F32 = jnp.float32
BF16 = jnp.bfloat16


def dot(a, b):
    return jnp.dot(a, b, preferred_element_type=F32)


def dot_nt(a, b):
    return lax.dot_general(a, b, (((1,), (1,)), ((), ())), preferred_element_type=F32)


def dot_tn(a, b):
    return lax.dot_general(a, b, (((0,), (0,)), ((), ())), preferred_element_type=F32)


def tile(c, width=TILE):
    return pl.ds(pl.multiple_of(c * width, width), width)


def loop(count, body):
    lax.fori_loop(0, count, lambda i, _: (body(i), 0)[1], 0)


def hadamard_pair():
    i = lax.broadcasted_iota(jnp.int32, (2 * HB, 2 * HB), 0)
    j = lax.broadcasted_iota(jnp.int32, (2 * HB, 2 * HB), 1)
    c = i & j & (HB - 1)
    c = c ^ (c >> 4)
    c = c ^ (c >> 2)
    c = c ^ (c >> 1)
    value = (1 - 2 * (c & 1)).astype(F32)
    return jnp.where((i >> 7) == (j >> 7), value, 0.0).astype(BF16)


def kernel(
    roster, bits, gain, fin, sav, gin, wq, wk, wv, wo,
    of, ob,
    fv, sv, gv, wqv, wkv, wov, fr, sr, gr,
    had, rows_scale, qv, kvv, ctx, dctx, dq, dkv, dkvb,
    ra_f, rbx_f, rbz_f, ra_b, rbx_b, rbz_b, total, stage_f, stage_b,
    load, send, recv,
):
    p = lax.axis_index("pipe")
    t = lax.axis_index("tensor")
    x = lax.rem(t, 2)
    z = lax.div(t, 2)
    n_pipe = lax.axis_size("pipe")
    zp, z2, zm = lax.rem(z + 1, 4), lax.rem(z + 2, 4), lax.rem(z + 3, 4)
    par = lax.rem(p, 2)
    swap = 1 - 2 * x
    up, down, side = (p, zp * 2 + x), (p, zm * 2 + x), (p, t + swap)
    after = (lax.rem(p + 1, n_pipe), t + par * swap)
    before = (lax.rem(p + n_pipe - 1, n_pipe), t + (1 - par) * swap)
    held_f = t + (1 - par) * swap
    held_b = t + par * swap

    def block(index):
        return pl.ds(pl.multiple_of(index * BLOCK, BLOCK), BLOCK)

    mine = block(t)
    loads = [
        (fin, fv), (wk, wkv.at[:, :, pl.ds(0, HD)]), (wv, wkv.at[:, :, pl.ds(HD, HD)]), (wq, wqv), (wo, wov),
        (sav, sv), (gin, gv), (fin.at[mine], fr), (sav.at[mine], sr), (gin.at[mine], gr),
    ]
    loads = [pltpu.make_async_copy(a, b, load.at[i]) for i, (a, b) in enumerate(loads)]
    for one in loads:
        one.start()
    l_fin, l_wk, l_wv, l_wq, l_wo, l_sav, l_gin, l_fr, l_sr, l_gr = loads

    barrier = pltpu.get_barrier_semaphore()
    for other in (up, down, side, after, before):
        pl.semaphore_signal(barrier, inc=1, device_id=other, device_id_type=MESH)

    front, back = roster[0], roster[1]
    had[...] = hadamard_pair()

    def signs(cols):
        return (2 * bits[:, cols] - 1).astype(F32)

    counter = [0]
    started = []

    def push(src, dst, device):
        i = counter[0]
        counter[0] += 1
        copy = pltpu.make_async_remote_copy(
            src_ref=src, dst_ref=dst, send_sem=send.at[i], recv_sem=recv.at[i], device_id=device, device_id_type=MESH
        )
        copy.start()
        started.append(copy)
        return copy

    def scales(ref):
        def body(i):
            rows = tile(i, 32)
            v = ref[rows, :].astype(F32)
            s = lax.rsqrt(jnp.sum(v * v, axis=-1, keepdims=True) * (1.0 / D) + EPS)
            rows_scale[rows, :] = jnp.broadcast_to(s, (32, 128))
        loop(ROWS // 32, body)

    def project(ref, which):
        kvv[...] = dot(ref[...], wkv[which]).astype(BF16)
        def body(n):
            cols = tile(n)
            qv[:, cols] = dot(ref[...], wqv[which, :, cols]).astype(BF16)
        return body

    def probabilities(q, lo, size):
        n = lo + size
        s = dot_nt(q, kvv[pl.ds(0, n), pl.ds(0, HD)]) * SM
        row = lax.broadcasted_iota(jnp.int32, (size, n), 0) + lo
        col = lax.broadcasted_iota(jnp.int32, (size, n), 1)
        s = jnp.where(row >= col, s, -1e30)
        e = jnp.exp(s - jnp.max(s, axis=-1, keepdims=True))
        return e / jnp.sum(e, axis=-1, keepdims=True)

    def add(ref, base, cols, *terms):
        def body(i):
            rows = pl.ds(pl.multiple_of(base * BLOCK + i * 16, 16), 16)
            value = ref[rows, cols].astype(F32)
            for term in terms:
                value += term[pl.ds(pl.multiple_of(i * 16, 16), 16), :].astype(F32)
            ref[rows, cols] = value.astype(BF16)
        loop(BLOCK // 16, body)

    def scatter(part, ra, rbx, rbz, whole):
        c = {}

        def first_a():
            c["m0"] = push(part.at[block(2 * z2), A], ra.at[0], up)
            c["p0"] = push(part.at[block(2 * z2 + 1), A], ra.at[1], down)
            c["m1"] = push(part.at[block(2 * zp + 1), A], ra.at[2], up)
            c["p1"] = push(part.at[block(2 * zm), A], ra.at[3], down)

        def first_b():
            for k, zz in ((2, z2), (1, zp), (3, zm), (0, z)):
                c["x", k] = push(part.at[block(2 * zz + 1 - x), B], rbx.at[k], side)

        def s1():
            c["m0"].wait_recv()
            add(part, 2 * zp, A, ra.at[0])
            c["m2"] = push(part.at[block(2 * zp), A], ra.at[4], up)
            c["p0"].wait_recv()
            add(part, 2 * zm + 1, A, ra.at[1])
            c["p2"] = push(part.at[block(2 * zm + 1), A], ra.at[5], down)
            c["x", 2].wait_recv()
            add(part, 2 * z2 + x, B, rbx.at[2])
            c["bm0"] = push(part.at[block(2 * z2 + x), BL], rbz.at[0], up)
            c["bp0"] = push(part.at[block(2 * z2 + x), BR], rbz.at[1], down)

        def s2():
            c["x", 1].wait_recv()
            add(part, 2 * zp + x, B, rbx.at[1])
            c["bm1"] = push(part.at[block(2 * zp + x), BR], rbz.at[2], up)
            c["x", 3].wait_recv()
            add(part, 2 * zm + x, B, rbx.at[3])
            c["bp1"] = push(part.at[block(2 * zm + x), BL], rbz.at[3], down)
            c["bm0"].wait_recv()
            add(part, 2 * zp + x, BL, rbz.at[0])
            c["bm2"] = push(part.at[block(2 * zp + x), BL], rbz.at[4], up)
            c["bp0"].wait_recv()
            add(part, 2 * zm + x, BR, rbz.at[1])
            c["bp2"] = push(part.at[block(2 * zm + x), BR], rbz.at[5], down)

        def s3():
            for name in ("m1", "m2", "p1", "p2"):
                c[name].wait_recv()
            add(part, 2 * z + 1 - x, A, ra.at[2 + 2 * x], ra.at[5 - 2 * x])
            c["ax"] = push(part.at[block(2 * z + 1 - x), A], ra.at[6], side)

        def s4():
            for name in ("ax", ("x", 0), "bm1", "bm2", "bp1", "bp2"):
                c[name].wait_recv()

            def body(i):
                rows = tile(i, 16)
                own = pl.ds(pl.multiple_of(t * BLOCK + i * 16, 16), 16)
                get = lambda ref, *at: ref[at].astype(F32)
                whole[rows, A] = (
                    get(part, own, A) + get(ra, 4 - 2 * x, rows) + get(ra, 3 + 2 * x, rows) + get(ra, 6, rows)
                )
                whole[rows, BL] = (
                    get(part, own, BL) + get(rbx, 0, rows, pl.ds(0, HALF)) + get(rbz, 4, rows) + get(rbz, 3, rows)
                )
                whole[rows, BR] = (
                    get(part, own, BR) + get(rbx, 0, rows, pl.ds(HALF, HALF)) + get(rbz, 2, rows) + get(rbz, 5, rows)
                )
            loop(BLOCK // 16, body)

        return first_a, first_b, s1, s2, s3, s4

    def turn(whole, held, stage):
        def body(n):
            cols = tile(n)
            v = whole[:, cols] * signs(cols)
            hi = v.astype(BF16)
            lo = (v - hi.astype(F32)).astype(BF16)
            y = dot(hi, had[...]) + dot(lo, had[...])
            stage[:, cols] = (held[:, cols].astype(F32) + y * UNIT).astype(BF16)
        loop(D // TILE, body)

    def gather(out, stage, device, r):
        c = {}
        rx = lax.rem(r, 2)

        def go(zz, xx, cols, device):
            here = out.at[block(2 * zz + xx), cols]
            return push(here, here, device)

        def shift():
            c["s"] = push(stage, out.at[mine], device)

        def g1():
            c["s"].wait_recv()
            c["ax"] = go(z, rx, A, side)
            c["bm0"] = go(z, rx, B, up)
            c["bp0"] = go(z, rx, B, down)
            c["am0"] = go(z, rx, A, up)
            c["ap0"] = go(z, rx, A, down)
            c["bx0"] = go(z, rx, B, side)

        def g2():
            c["bm0"].wait_recv()
            c["bm1"] = go(zm, rx, BL, up)
            c["bx1"] = go(zm, rx, B, side)
            c["bp0"].wait_recv()
            c["bp1"] = go(zp, rx, BR, down)
            c["bx2"] = go(zp, rx, B, side)
            c["ax"].wait_recv()
            c["am1"] = go(z, 1 - rx, A, up)
            c["ap1"] = go(z, 1 - rx, A, down)
            c["am0"].wait_recv()
            c["am2"] = go(zm, rx, A, up)

        def g3():
            c["bm1"].wait_recv()
            c["bx3"] = go(z2, rx, BL, side)
            c["bp1"].wait_recv()
            c["bx4"] = go(z2, rx, BR, side)
            c["ap1"].wait_recv()
            c["ap2"] = go(zp, 1 - rx, A, down)

        def g4():
            for name in ("ap0", "am1", "am2", "ap2", "bx0", "bx1", "bx2", "bx3", "bx4"):
                c[name].wait_recv()

        return shift, g1, g2, g3, g4

    fa, fb, fs1, fs2, fs3, fs4 = scatter(fv, ra_f, rbx_f, rbz_f, total)
    ba, bb, bs1, bs2, bs3, bs4 = scatter(sv, ra_b, rbx_b, rbz_b, total)
    f_shift, fg1, fg2, fg3, fg4 = gather(of, stage_f, after, held_f)
    b_shift, bg1, bg2, bg3, bg4 = gather(ob, stage_b, before, held_b)

    l_fin.wait()
    scales(fv)

    def normed_front(n):
        cols = tile(n)
        y = dot(fv[:, cols], had[...])
        column = signs(cols) * gain[pl.ds(front, 1), cols] * UNIT
        s = rows_scale[...]
        fv[:, cols] = (y * column * jnp.concatenate([s, s], axis=1)).astype(BF16)
    loop(D // TILE, normed_front)
    l_wk.wait()
    l_wv.wait()
    q_step = project(fv, front)
    l_wq.wait()
    loop(2, q_step)

    def attend(h):
        cols = tile(h, HD)
        for lo in (0, 256):
            rows = pl.ds(lo, 256)
            probs = probabilities(qv[rows, cols], lo, 256).astype(BF16)
            ctx[rows, cols] = dot(probs, kvv[pl.ds(0, lo + 256), pl.ds(HD, HD)]).astype(BF16)
    loop(HEADS, attend)
    l_wo.wait()

    def project_out(n):
        cols = tile(n)
        fv[:, cols] = dot(ctx[...], wov[front, :, cols]).astype(BF16)
    loop(CA // TILE, project_out)
    pl.semaphore_wait(barrier, 5)
    fa()
    loop(CB // TILE, lambda n: project_out(n + CA // TILE))
    fb()

    l_sav.wait()
    scales(sv)

    def normed_back(n):
        cols = tile(n)
        s = rows_scale[...]
        sv[:, cols] = (
            sv[:, cols].astype(F32) * gain[pl.ds(back, 1), cols] * jnp.concatenate([s, s], axis=1)
        ).astype(BF16)
    loop(D // TILE, normed_back)
    q_step = project(sv, back)
    loop(2, q_step)
    fs1()
    l_gin.wait()

    def unrotated(n):
        cols = tile(n)
        gv[:, cols] = (dot(gv[:, cols], had[...]) * (signs(cols) * UNIT)).astype(BF16)
    loop(D // TILE, unrotated)

    def pull_out(n):
        rows = tile(n)
        dctx[:, rows] = dot_nt(gv[...], wov[back, rows, :]).astype(BF16)
    loop(2, pull_out)
    dkv[...] = jnp.zeros_like(dkv)

    def attend_back(h):
        cols = tile(h, HD)
        for lo in (0, 256):
            rows, n = pl.ds(lo, 256), pl.ds(0, lo + 256)
            q, d = qv[rows, cols], dctx[rows, cols]
            probs = probabilities(q, lo, 256)
            dkv[n, pl.ds(HD, HD)] += dot_tn(probs.astype(BF16), d)
            dp = dot_nt(d, kvv[n, pl.ds(HD, HD)])
            ds = probs * (dp - jnp.sum(probs * dp, axis=-1, keepdims=True)) * SM
            ds = ds.astype(BF16)
            dq[rows, cols] = dot(ds, kvv[n, pl.ds(0, HD)]).astype(BF16)
            dkv[n, pl.ds(0, HD)] += dot_tn(ds, q)
    loop(HEADS, attend_back)
    dkvb[...] = dkv[...].astype(BF16)
    fs2()

    def pull_in(n):
        cols = tile(n)
        sv[:, cols] = (dot_nt(dq[...], wqv[back, cols, :]) + dot_nt(dkvb[...], wkv[back, cols, :])).astype(BF16)
    loop(CA // TILE, pull_in)
    ba()
    loop(CB // TILE, lambda n: pull_in(n + CA // TILE))
    bb()

    fs3()
    bs1()
    fs4()
    l_fr.wait()
    turn(total, fr, stage_f)
    f_shift()
    bs2()
    fg1()
    bs3()
    fg2()
    bs4()
    l_sr.wait()
    l_gr.wait()

    def norm_back(i):
        rows = tile(i, 16)
        v = sr[rows, :].astype(F32)
        s = lax.rsqrt(jnp.sum(v * v, axis=-1, keepdims=True) * (1.0 / D) + EPS)
        g = total[rows, :] * gain[pl.ds(back, 1), :]
        inner = jnp.sum(v * g, axis=-1, keepdims=True)
        total[rows, :] = s * g - v * (s * s * s * inner * (1.0 / D))
    loop(BLOCK // 16, norm_back)
    turn(total, gr, stage_b)
    b_shift()
    fg3()
    bg1()
    fg4()
    bg2()
    bg3()
    bg4()
    for copy in started:
        copy.wait_send()


def local(forward_input, saved_input, gradient_input, roster, sign_bits, gain, w_query, w_key, w_value, w_out):
    vm = lambda shape, kind=BF16: pltpu.VMEM(shape, kind)
    anywhere = pl.BlockSpec(memory_space=pl.ANY)
    inside = pl.BlockSpec(memory_space=pltpu.VMEM)
    sums = [vm((7, BLOCK, CA)), vm((4, BLOCK, CB)), vm((6, BLOCK, HALF))]
    out = jax.ShapeDtypeStruct((ROWS, D), BF16)
    arrived, returned = pl.pallas_call(
        kernel,
        out_shape=(out, out),
        in_specs=[pl.BlockSpec(memory_space=pltpu.SMEM), inside, inside] + [anywhere] * 7,
        out_specs=(anywhere, anywhere),
        scratch_shapes=[
            vm((ROWS, D)), vm((ROWS, D)), vm((ROWS, D)),
            vm((2, D, HEADS * HD)), vm((2, D, 2 * HD)), vm((2, HEADS * HD, D)),
            vm((BLOCK, D)), vm((BLOCK, D)), vm((BLOCK, D)),
            vm((2 * HB, 2 * HB)), vm((ROWS, 128), F32),
            vm((ROWS, HEADS * HD)), vm((ROWS, 2 * HD)), vm((ROWS, HEADS * HD)), vm((ROWS, HEADS * HD)),
            vm((ROWS, HEADS * HD)), vm((ROWS, 2 * HD), F32), vm((ROWS, 2 * HD)),
            *sums, *sums, vm((BLOCK, D), F32), vm((BLOCK, D)), vm((BLOCK, D)),
            pltpu.SemaphoreType.DMA((10,)), pltpu.SemaphoreType.DMA((68,)), pltpu.SemaphoreType.DMA((68,)),
        ],
        compiler_params=pltpu.CompilerParams(
            collective_id=0, has_side_effects=True, vmem_limit_bytes=60 * 2**20
        ),
        cost_estimate=pl.CostEstimate(flops=16 * 10**9, bytes_accessed=45 * 10**6, transcendentals=2 * 10**6),
        name="relay_slot",
    )(
        roster[0], sign_bits[None], gain[0], forward_input[0], saved_input[0], gradient_input[0],
        w_query[0], w_key[0], w_value[0], w_out[0],
    )
    return (arrived[None], returned[None])


def solution(mesh):
    placed = (
        P("pipe", None, None),
        P("pipe", None, None),
        P("pipe", None, None),
        P("pipe", None),
        P(),
        P("pipe", None, None),
        P("pipe", None, None, "tensor"),
        P("pipe", None, None, "tensor"),
        P("pipe", None, None, "tensor"),
        P("pipe", None, "tensor", None),
    )
    return jax.shard_map(
        local,
        mesh=mesh,
        in_specs=placed,
        out_specs=(P("pipe", None, None), P("pipe", None, None)),
        check_vma=False,
    )
```

```python
import functools
import math

import jax
import jax.numpy as jnp
from jax import lax
from jax.experimental import pallas as pl
from jax.experimental.pallas import tpu as pltpu
from jax.sharding import PartitionSpec as P

MESH = pl.DeviceIdType.MESH
D = 4096
ROWS = 512
HD = 128
HB = 128
HEADS = 4
BLOCK = 64
CA = 2304
CB = D - CA
HALF = CB // 2
TILE = 256
EPS = 1e-05
UNIT = 1.0 / math.sqrt(HB)
SM = 1.0 / math.sqrt(HD)
A = pl.ds(0, CA)
B = pl.ds(CA, CB)
BL = pl.ds(CA, HALF)
BR = pl.ds(CA + HALF, HALF)
F32 = jnp.float32
BF16 = jnp.bfloat16


def dot(a, b):
    return jnp.dot(a, b, preferred_element_type=F32)


def dot_nt(a, b):
    return lax.dot_general(a, b, (((1,), (1,)), ((), ())), preferred_element_type=F32)


def dot_tn(a, b):
    return lax.dot_general(a, b, (((0,), (0,)), ((), ())), preferred_element_type=F32)


def tile(c, width=TILE):
    return pl.ds(pl.multiple_of(c * width, width), width)


def loop(count, body, unroll=1, start=0):
    lax.fori_loop(start, start + count, lambda i, _: (body(i), 0)[1], 0, unroll=unroll)


def hadamard_pair():
    i = lax.broadcasted_iota(jnp.int32, (2 * HB, 2 * HB), 0)
    j = lax.broadcasted_iota(jnp.int32, (2 * HB, 2 * HB), 1)
    c = i & j & (HB - 1)
    c = c ^ (c >> 4)
    c = c ^ (c >> 2)
    c = c ^ (c >> 1)
    value = (1 - 2 * (c & 1)).astype(F32)
    return jnp.where((i >> 7) == (j >> 7), value, 0.0).astype(BF16)


def kernel(
    roster, bits, gain, fin, sav, gin, wq, wk, wv, wo,
    of, ob,
    fv, sv, gv, wqv, wkv, wov, fr, sr, gr,
    had, rows_scale, qv, kvv, ctx, dctx, dq, dkv, dkvb,
    ra_f, rbx_f, rbz_f, ra_b, rbx_b, rbz_b, total, stage_f, stage_b,
    load, send, recv,
):
    p = lax.axis_index("pipe")
    t = lax.axis_index("tensor")
    x = lax.rem(t, 2)
    z = lax.div(t, 2)
    n_pipe = lax.axis_size("pipe")
    zp, z2, zm = lax.rem(z + 1, 4), lax.rem(z + 2, 4), lax.rem(z + 3, 4)
    par = lax.rem(p, 2)
    swap = 1 - 2 * x
    up, down, side = (p, zp * 2 + x), (p, zm * 2 + x), (p, t + swap)
    after = (lax.rem(p + 1, n_pipe), t + par * swap)
    before = (lax.rem(p + n_pipe - 1, n_pipe), t + (1 - par) * swap)
    held_f = t + (1 - par) * swap
    held_b = t + par * swap

    def block(index):
        return pl.ds(pl.multiple_of(index * BLOCK, BLOCK), BLOCK)

    mine = block(t)
    loads = [
        (wk, wkv.at[:, :, pl.ds(0, HD)]), (wv, wkv.at[:, :, pl.ds(HD, HD)]), (wq, wqv), (wo, wov),
        (sav, sv), (gin, gv), (fin.at[mine], fr), (sav.at[mine], sr), (gin.at[mine], gr),
    ]
    quarters = [pl.ds(i * 128, 128) for i in range(4)]
    loads += [(fin.at[rows], fv.at[rows]) for rows in quarters]
    loads = [pltpu.make_async_copy(a, b, load.at[i]) for i, (a, b) in enumerate(loads)]
    l_wk, l_wv, l_wq, l_wo, l_sav, l_gin, l_fr, l_sr, l_gr, *l_fin = loads
    for one in (*l_fin, l_wk, l_wv, l_wq):
        one.start()

    barrier = pltpu.get_barrier_semaphore()
    for other in (up, down, side, after, before):
        pl.semaphore_signal(barrier, inc=1, device_id=other, device_id_type=MESH)

    front, back = roster[0], roster[1]
    had[...] = hadamard_pair()

    def signs(cols):
        return (2 * bits[:, cols] - 1).astype(F32)

    counter = [0]
    started = []

    def push(src, dst, device):
        i = counter[0]
        counter[0] += 1
        copy = pltpu.make_async_remote_copy(
            src_ref=src, dst_ref=dst, send_sem=send.at[i], recv_sem=recv.at[i], device_id=device, device_id_type=MESH
        )
        copy.start()
        started.append(copy)
        return copy

    def scales(factor):
        total_square = jnp.sum(rows_scale[...], axis=-1, keepdims=True)
        rows_scale[...] = jnp.broadcast_to(lax.rsqrt(total_square * (factor / D) + EPS), (ROWS, 128))

    def project(ref, which):
        s = rows_scale[...]
        s2 = jnp.concatenate([s, s], axis=1)
        kvv[...] = (dot(ref[...], wkv[which]) * s2).astype(BF16)
        for n in range(2):
            cols = pl.ds(n * TILE, TILE)
            qv[:, cols] = (dot(ref[...], wqv[which, :, cols]) * (s2 * SM)).astype(BF16)

    def weights(q, lo, size):
        n = lo + size
        s = dot_nt(q, kvv[pl.ds(0, n), pl.ds(0, HD)])
        row = lax.broadcasted_iota(jnp.int32, (size, n), 0) + lo
        col = lax.broadcasted_iota(jnp.int32, (size, n), 1)
        s = jnp.where(row >= col, s, -1e30)
        e = jnp.exp(s - jnp.max(s, axis=-1, keepdims=True))
        return e, 1.0 / jnp.sum(e, axis=-1, keepdims=True)

    def add(ref, base, cols, *terms):
        def body(i):
            rows = pl.ds(pl.multiple_of(base * BLOCK + i * 16, 16), 16)
            value = ref[rows, cols].astype(F32)
            for term in terms:
                value += term[pl.ds(pl.multiple_of(i * 16, 16), 16), :].astype(F32)
            ref[rows, cols] = value.astype(BF16)
        loop(BLOCK // 16, body)

    def scatter(part, ra, rbx, rbz, whole):
        c = {}

        def first_a():
            c["m0"] = push(part.at[block(2 * z2), A], ra.at[0], up)
            c["p0"] = push(part.at[block(2 * z2 + 1), A], ra.at[1], down)
            c["m1"] = push(part.at[block(2 * zp + 1), A], ra.at[2], up)
            c["p1"] = push(part.at[block(2 * zm), A], ra.at[3], down)

        def first_b():
            for k, zz in ((2, z2), (1, zp), (3, zm), (0, z)):
                c["x", k] = push(part.at[block(2 * zz + 1 - x), B], rbx.at[k], side)

        def s1():
            c["m0"].wait_recv()
            add(part, 2 * zp, A, ra.at[0])
            c["m2"] = push(part.at[block(2 * zp), A], ra.at[4], up)
            c["p0"].wait_recv()
            add(part, 2 * zm + 1, A, ra.at[1])
            c["p2"] = push(part.at[block(2 * zm + 1), A], ra.at[5], down)

        def s1x():
            c["x", 2].wait_recv()
            add(part, 2 * z2 + x, B, rbx.at[2])
            c["bm0"] = push(part.at[block(2 * z2 + x), BL], rbz.at[0], up)
            c["bp0"] = push(part.at[block(2 * z2 + x), BR], rbz.at[1], down)

        def s2():
            c["x", 1].wait_recv()
            add(part, 2 * zp + x, B, rbx.at[1])
            c["bm1"] = push(part.at[block(2 * zp + x), BR], rbz.at[2], up)
            c["bm0"].wait_recv()
            add(part, 2 * zp + x, BL, rbz.at[0])
            c["bm2"] = push(part.at[block(2 * zp + x), BL], rbz.at[4], up)

        def s2x():
            c["x", 3].wait_recv()
            add(part, 2 * zm + x, B, rbx.at[3])
            c["bp1"] = push(part.at[block(2 * zm + x), BL], rbz.at[3], down)
            c["bp0"].wait_recv()
            add(part, 2 * zm + x, BR, rbz.at[1])
            c["bp2"] = push(part.at[block(2 * zm + x), BR], rbz.at[5], down)

        def s3():
            for name in ("m1", "m2", "p1", "p2"):
                c[name].wait_recv()
            add(part, 2 * z + 1 - x, A, ra.at[2 + 2 * x], ra.at[5 - 2 * x])
            c["ax"] = push(part.at[block(2 * z + 1 - x), A], ra.at[6], side)

        def s4():
            for name in ("ax", ("x", 0), "bm1", "bm2", "bp1", "bp2"):
                c[name].wait_recv()

            def body(i):
                rows = tile(i, 16)
                own = pl.ds(pl.multiple_of(t * BLOCK + i * 16, 16), 16)
                get = lambda ref, *at: ref[at].astype(F32)
                whole[rows, A] = (
                    get(part, own, A) + get(ra, 4 - 2 * x, rows) + get(ra, 3 + 2 * x, rows) + get(ra, 6, rows)
                )
                whole[rows, BL] = (
                    get(part, own, BL) + get(rbx, 0, rows, pl.ds(0, HALF)) + get(rbz, 4, rows) + get(rbz, 3, rows)
                )
                whole[rows, BR] = (
                    get(part, own, BR) + get(rbx, 0, rows, pl.ds(HALF, HALF)) + get(rbz, 2, rows) + get(rbz, 5, rows)
                )
            loop(BLOCK // 16, body)

        return first_a, first_b, s1, s1x, s2, s2x, s3, s4

    def turn(whole, held, stage):
        def body(n):
            cols = tile(n)
            v = whole[:, cols] * signs(cols)
            hi = v.astype(BF16)
            lo = (v - hi.astype(F32)).astype(BF16)
            y = dot(hi, had[...]) + dot(lo, had[...])
            stage[:, cols] = (held[:, cols].astype(F32) + y * UNIT).astype(BF16)
        loop(D // TILE, body, 4)

    def gather(out, stage, device, r):
        c = {}
        rx = lax.rem(r, 2)

        def go(zz, xx, cols, device):
            here = out.at[block(2 * zz + xx), cols]
            return push(here, here, device)

        def shift():
            c["s"] = push(stage, out.at[mine], device)

        def g1():
            c["s"].wait_recv()
            c["ax"] = go(z, rx, A, side)
            c["bm0"] = go(z, rx, B, up)
            c["bp0"] = go(z, rx, B, down)
            c["am0"] = go(z, rx, A, up)
            c["ap0"] = go(z, rx, A, down)
            c["bx0"] = go(z, rx, B, side)

        def g2():
            c["bm0"].wait_recv()
            c["bm1"] = go(zm, rx, BL, up)
            c["bx1"] = go(zm, rx, B, side)
            c["bp0"].wait_recv()
            c["bp1"] = go(zp, rx, BR, down)
            c["bx2"] = go(zp, rx, B, side)
            c["ax"].wait_recv()
            c["am1"] = go(z, 1 - rx, A, up)
            c["ap1"] = go(z, 1 - rx, A, down)
            c["am0"].wait_recv()
            c["am2"] = go(zm, rx, A, up)

        def g3():
            c["bm1"].wait_recv()
            c["bx3"] = go(z2, rx, BL, side)
            c["bp1"].wait_recv()
            c["bx4"] = go(z2, rx, BR, side)
            c["ap1"].wait_recv()
            c["ap2"] = go(zp, 1 - rx, A, down)

        def g4():
            for name in ("ap0", "am1", "am2", "ap2", "bx0", "bx1", "bx2", "bx3", "bx4"):
                c[name].wait_recv()

        return shift, g1, g2, g3, g4

    fa, fb, fs1, fs1x, fs2, fs2x, fs3, fs4 = scatter(fv, ra_f, rbx_f, rbz_f, total)
    ba, bb, bs1, bs1x, bs2, bs2x, bs3, bs4 = scatter(sv, ra_b, rbx_b, rbz_b, total)
    f_shift, fg1, fg2, fg3, fg4 = gather(of, stage_f, after, held_f)
    b_shift, bg1, bg2, bg3, bg4 = gather(ob, stage_b, before, held_b)

    rows_scale[...] = jnp.zeros_like(rows_scale)
    for one in l_fin:
        one.wait()
    l_wo.start()

    def weighted_front(n):
        cols = tile(n)
        y = dot(fv[:, cols], had[...])
        fv[:, cols] = (y * (signs(cols) * gain[pl.ds(front, 1), cols] * UNIT)).astype(BF16)
        y = y * y
        rows_scale[...] += y[:, :128] + y[:, 128:]
    loop(D // TILE, weighted_front, 4)
    scales(1.0 / HB)
    l_wk.wait()
    l_wv.wait()
    l_wq.wait()
    for one in (l_sav, l_gin, l_fr, l_sr, l_gr):
        one.start()
    project(fv, front)

    for h in range(HEADS):
        cols = pl.ds(h * HD, HD)
        for lo in (0, 256):
            rows = pl.ds(lo, 256)
            e, r = weights(qv[rows, cols], lo, 256)
            ctx[rows, cols] = (dot(e.astype(BF16), kvv[pl.ds(0, lo + 256), pl.ds(HD, HD)]) * r).astype(BF16)
    l_wo.wait()

    def project_out(n):
        cols = tile(n)
        fv[:, cols] = dot(ctx[...], wov[front, :, cols]).astype(BF16)
    loop(CA // TILE, project_out, 3)
    pl.semaphore_wait(barrier, 5)
    fa()
    loop(CB // TILE, project_out, 7, CA // TILE)
    fb()

    rows_scale[...] = jnp.zeros_like(rows_scale)
    l_sav.wait()

    def weighted_back(n):
        cols = tile(n)
        v = sv[:, cols].astype(F32)
        sv[:, cols] = (v * gain[pl.ds(back, 1), cols]).astype(BF16)
        v = v * v
        rows_scale[...] += v[:, :128] + v[:, 128:]
    loop(D // TILE, weighted_back, 4)
    scales(1.0)
    project(sv, back)
    fs1()
    fs1x()
    l_gin.wait()

    def unrotated(n):
        cols = tile(n)
        gv[:, cols] = (dot(gv[:, cols], had[...]) * (signs(cols) * UNIT)).astype(BF16)
    loop(D // TILE, unrotated, 4)

    for n in range(2):
        rows = pl.ds(n * TILE, TILE)
        dctx[:, rows] = dot_nt(gv[...], wov[back, rows, :]).astype(BF16)
    fs2()
    dkv[...] = jnp.zeros_like(dkv)

    def attend_back(h):
        cols = pl.ds(h * HD, HD)
        for lo in (0, 256):
            rows, n = pl.ds(lo, 256), pl.ds(0, lo + 256)
            q, d = qv[rows, cols], dctx[rows, cols]
            e, r = weights(q, lo, 256)
            probs = e * r
            dkv[pl.ds(HD, HD), n] += dot_tn(d, probs.astype(BF16))
            dp = dot_nt(d, kvv[n, pl.ds(HD, HD)])
            ds = (probs * (dp - jnp.sum(probs * dp, axis=-1, keepdims=True))).astype(BF16)
            dq[rows, cols] = (dot(ds, kvv[n, pl.ds(0, HD)]) * SM).astype(BF16)
            dkv[pl.ds(0, HD), n] += dot_tn(q, ds)
    attend_back(0)
    attend_back(1)
    fs2x()
    attend_back(2)
    attend_back(3)
    dkvb[...] = dkv[...].astype(BF16)
    fs3()

    def pull_in(n):
        cols = tile(n)
        sv[:, cols] = (dot_nt(dq[...], wqv[back, cols, :]) + dot_nt(dkvb[...].T, wkv[back, cols, :])).astype(BF16)
    loop(CA // TILE, pull_in, 3)
    ba()
    loop(CB // TILE, pull_in, 7, CA // TILE)
    bb()

    fs4()
    l_fr.wait()
    turn(total, fr, stage_f)
    f_shift()
    bs1()
    bs1x()
    bs2()
    fg1()
    bs2x()
    fg2()
    bs3()
    fg3()
    bs4()
    l_sr.wait()
    l_gr.wait()

    def norm_back(i):
        rows = tile(i, 16)
        v = sr[rows, :].astype(F32)
        s = lax.rsqrt(jnp.sum(v * v, axis=-1, keepdims=True) * (1.0 / D) + EPS)
        g = total[rows, :] * gain[pl.ds(back, 1), :]
        inner = jnp.sum(v * g, axis=-1, keepdims=True)
        total[rows, :] = s * g - v * (s * s * s * inner * (1.0 / D))
    loop(BLOCK // 16, norm_back)
    turn(total, gr, stage_b)
    b_shift()
    bg1()
    fg4()
    bg2()
    bg3()
    bg4()
    for copy in started:
        copy.wait_send()


def local(forward_input, saved_input, gradient_input, roster, sign_bits, gain, w_query, w_key, w_value, w_out):
    vm = lambda shape, kind=BF16: pltpu.VMEM(shape, kind)
    anywhere = pl.BlockSpec(memory_space=pl.ANY)
    inside = pl.BlockSpec(memory_space=pltpu.VMEM)
    sums = [vm((7, BLOCK, CA)), vm((4, BLOCK, CB)), vm((6, BLOCK, HALF))]
    out = jax.ShapeDtypeStruct((ROWS, D), BF16)
    arrived, returned = pl.pallas_call(
        kernel,
        out_shape=(out, out),
        in_specs=[pl.BlockSpec(memory_space=pltpu.SMEM), inside, inside] + [anywhere] * 7,
        out_specs=(anywhere, anywhere),
        scratch_shapes=[
            vm((ROWS, D)), vm((ROWS, D)), vm((ROWS, D)),
            vm((2, D, HEADS * HD)), vm((2, D, 2 * HD)), vm((2, HEADS * HD, D)),
            vm((BLOCK, D)), vm((BLOCK, D)), vm((BLOCK, D)),
            vm((2 * HB, 2 * HB)), vm((ROWS, 128), F32),
            vm((ROWS, HEADS * HD)), vm((ROWS, 2 * HD)), vm((ROWS, HEADS * HD)), vm((ROWS, HEADS * HD)),
            vm((ROWS, HEADS * HD)), vm((2 * HD, ROWS), F32), vm((2 * HD, ROWS)),
            *sums, *sums, vm((BLOCK, D), F32), vm((BLOCK, D)), vm((BLOCK, D)),
            pltpu.SemaphoreType.DMA((13,)), pltpu.SemaphoreType.DMA((68,)), pltpu.SemaphoreType.DMA((68,)),
        ],
        compiler_params=pltpu.CompilerParams(
            collective_id=0, has_side_effects=True, vmem_limit_bytes=60 * 2**20
        ),
        cost_estimate=pl.CostEstimate(flops=16 * 10**9, bytes_accessed=45 * 10**6, transcendentals=2 * 10**6),
        name="relay_slot",
    )(
        roster[0], sign_bits[None], gain[0], forward_input[0], saved_input[0], gradient_input[0],
        w_query[0], w_key[0], w_value[0], w_out[0],
    )
    return (arrived[None], returned[None])


def solution(mesh):
    placed = (
        P("pipe", None, None),
        P("pipe", None, None),
        P("pipe", None, None),
        P("pipe", None),
        P(),
        P("pipe", None, None),
        P("pipe", None, None, "tensor"),
        P("pipe", None, None, "tensor"),
        P("pipe", None, None, "tensor"),
        P("pipe", None, "tensor", None),
    )
    return jax.shard_map(
        local,
        mesh=mesh,
        in_specs=placed,
        out_specs=(P("pipe", None, None), P("pipe", None, None)),
        check_vma=False,
    )
```

```python
import functools
import math

import jax
import jax.numpy as jnp
from jax import lax
from jax.experimental import pallas as pl
from jax.experimental.pallas import tpu as pltpu
from jax.sharding import PartitionSpec as P

MESH = pl.DeviceIdType.MESH
D = 4096
ROWS = 512
HD = 128
HB = 128
HEADS = 4
BLOCK = 64
CA = 2304
CB = D - CA
HALF = CB // 2
TILE = 256
EPS = 1e-05
UNIT = 1.0 / math.sqrt(HB)
SM = 1.0 / math.sqrt(HD)
A = pl.ds(0, CA)
B = pl.ds(CA, CB)
BL = pl.ds(CA, HALF)
BR = pl.ds(CA + HALF, HALF)
F32 = jnp.float32
BF16 = jnp.bfloat16


def dot(a, b):
    return jnp.dot(a, b, preferred_element_type=F32)


def dot_nt(a, b):
    return lax.dot_general(a, b, (((1,), (1,)), ((), ())), preferred_element_type=F32)


def dot_tn(a, b):
    return lax.dot_general(a, b, (((0,), (0,)), ((), ())), preferred_element_type=F32)


def tile(c, width=TILE):
    return pl.ds(pl.multiple_of(c * width, width), width)


def loop(count, body, unroll=1, start=0):
    lax.fori_loop(start, start + count, lambda i, _: (body(i), 0)[1], 0, unroll=unroll)


def hadamard_pair():
    i = lax.broadcasted_iota(jnp.int32, (2 * HB, 2 * HB), 0)
    j = lax.broadcasted_iota(jnp.int32, (2 * HB, 2 * HB), 1)
    c = i & j & (HB - 1)
    c = c ^ (c >> 4)
    c = c ^ (c >> 2)
    c = c ^ (c >> 1)
    value = (1 - 2 * (c & 1)).astype(F32)
    return jnp.where((i >> 7) == (j >> 7), value, 0.0).astype(BF16)


def kernel(
    roster, bits, gain, fin, sav, gin, wq, wk, wv, wo,
    of, ob,
    fv, sv, gv, wqv, wkv, wov, fr, sr, gr,
    had, rows_scale, qv, kvv, ctx, dctx, dq, dkv, dkvb,
    ra_f, rbx_f, rbz_f, ra_b, rbx_b, rbz_b, total, stage_f, stage_b,
    load, send, recv,
):
    p = lax.axis_index("pipe")
    t = lax.axis_index("tensor")
    x = lax.rem(t, 2)
    z = lax.div(t, 2)
    n_pipe = lax.axis_size("pipe")
    zp, z2, zm = lax.rem(z + 1, 4), lax.rem(z + 2, 4), lax.rem(z + 3, 4)
    par = lax.rem(p, 2)
    swap = 1 - 2 * x
    up, down, side = (p, zp * 2 + x), (p, zm * 2 + x), (p, t + swap)
    after = (lax.rem(p + 1, n_pipe), t + par * swap)
    before = (lax.rem(p + n_pipe - 1, n_pipe), t + (1 - par) * swap)
    held_f = t + (1 - par) * swap
    held_b = t + par * swap

    def block(index):
        return pl.ds(pl.multiple_of(index * BLOCK, BLOCK), BLOCK)

    mine = block(t)
    loads = [
        (wk, wkv.at[:, :, pl.ds(0, HD)]), (wv, wkv.at[:, :, pl.ds(HD, HD)]), (wq, wqv), (wo, wov),
        (sav, sv), (gin, gv), (fin.at[mine], fr), (sav.at[mine], sr), (gin.at[mine], gr),
    ]
    quarters = [pl.ds(i * 128, 128) for i in range(4)]
    loads += [(fin.at[rows], fv.at[rows]) for rows in quarters]
    loads = [pltpu.make_async_copy(a, b, load.at[i]) for i, (a, b) in enumerate(loads)]
    l_wk, l_wv, l_wq, l_wo, l_sav, l_gin, l_fr, l_sr, l_gr, *l_fin = loads
    for one in (*l_fin, l_wk, l_wv, l_wq):
        one.start()

    barrier = pltpu.get_barrier_semaphore()
    for other in (up, down, side, after, before):
        pl.semaphore_signal(barrier, inc=1, device_id=other, device_id_type=MESH)

    front, back = roster[0], roster[1]
    had[...] = hadamard_pair()

    def signs(cols):
        return (2 * bits[:, cols] - 1).astype(F32)

    counter = [0]
    started = []

    def push(src, dst, device):
        i = counter[0]
        counter[0] += 1
        copy = pltpu.make_async_remote_copy(
            src_ref=src, dst_ref=dst, send_sem=send.at[i], recv_sem=recv.at[i], device_id=device, device_id_type=MESH
        )
        copy.start()
        started.append(copy)
        return copy

    def scales(factor):
        total_square = jnp.sum(rows_scale[...], axis=-1, keepdims=True)
        rows_scale[...] = jnp.broadcast_to(lax.rsqrt(total_square * (factor / D) + EPS), (ROWS, 128))

    def project(ref, which):
        s = rows_scale[...]
        s2 = jnp.concatenate([s, s], axis=1)
        kvv[...] = (dot(ref[...], wkv[which]) * s2).astype(BF16)
        for n in range(2):
            cols = pl.ds(n * TILE, TILE)
            qv[:, cols] = (dot(ref[...], wqv[which, :, cols]) * (s2 * SM)).astype(BF16)

    def weights(q, lo, size):
        n = lo + size
        s = dot_nt(q, kvv[pl.ds(0, n), pl.ds(0, HD)])
        row = lax.broadcasted_iota(jnp.int32, (size, n), 0) + lo
        col = lax.broadcasted_iota(jnp.int32, (size, n), 1)
        s = jnp.where(row >= col, s, -1e30)
        e = jnp.exp(s - jnp.max(s, axis=-1, keepdims=True))
        return e, 1.0 / jnp.sum(e, axis=-1, keepdims=True)

    def add(ref, base, cols, *terms):
        def body(i):
            rows = pl.ds(pl.multiple_of(base * BLOCK + i * 16, 16), 16)
            value = ref[rows, cols].astype(F32)
            for term in terms:
                value += term[pl.ds(pl.multiple_of(i * 16, 16), 16), :].astype(F32)
            ref[rows, cols] = value.astype(BF16)
        loop(BLOCK // 16, body)

    def scatter(part, ra, rbx, rbz, whole):
        c = {}

        def first_a():
            c["m0"] = push(part.at[block(2 * z2), A], ra.at[0], up)
            c["p0"] = push(part.at[block(2 * z2 + 1), A], ra.at[1], down)
            c["m1"] = push(part.at[block(2 * zp + 1), A], ra.at[2], up)
            c["p1"] = push(part.at[block(2 * zm), A], ra.at[3], down)

        def first_b():
            for k, zz in ((2, z2), (1, zp), (3, zm), (0, z)):
                c["x", k] = push(part.at[block(2 * zz + 1 - x), B], rbx.at[k], side)

        def s1():
            c["m0"].wait_recv()
            add(part, 2 * zp, A, ra.at[0])
            c["m2"] = push(part.at[block(2 * zp), A], ra.at[4], up)
            c["p0"].wait_recv()
            add(part, 2 * zm + 1, A, ra.at[1])
            c["p2"] = push(part.at[block(2 * zm + 1), A], ra.at[5], down)

        def s1x():
            c["x", 2].wait_recv()
            add(part, 2 * z2 + x, B, rbx.at[2])
            c["bm0"] = push(part.at[block(2 * z2 + x), BL], rbz.at[0], up)
            c["bp0"] = push(part.at[block(2 * z2 + x), BR], rbz.at[1], down)

        def s2():
            c["x", 1].wait_recv()
            add(part, 2 * zp + x, B, rbx.at[1])
            c["bm1"] = push(part.at[block(2 * zp + x), BR], rbz.at[2], up)
            c["bm0"].wait_recv()
            add(part, 2 * zp + x, BL, rbz.at[0])
            c["bm2"] = push(part.at[block(2 * zp + x), BL], rbz.at[4], up)

        def s2x():
            c["x", 3].wait_recv()
            add(part, 2 * zm + x, B, rbx.at[3])
            c["bp1"] = push(part.at[block(2 * zm + x), BL], rbz.at[3], down)
            c["bp0"].wait_recv()
            add(part, 2 * zm + x, BR, rbz.at[1])
            c["bp2"] = push(part.at[block(2 * zm + x), BR], rbz.at[5], down)

        def s3():
            for name in ("m1", "m2", "p1", "p2"):
                c[name].wait_recv()
            add(part, 2 * z + 1 - x, A, ra.at[2 + 2 * x], ra.at[5 - 2 * x])
            c["ax"] = push(part.at[block(2 * z + 1 - x), A], ra.at[6], side)

        def s4():
            for name in ("ax", ("x", 0), "bm1", "bm2", "bp1", "bp2"):
                c[name].wait_recv()

            def body(i):
                rows = tile(i, 16)
                own = pl.ds(pl.multiple_of(t * BLOCK + i * 16, 16), 16)
                get = lambda ref, *at: ref[at].astype(F32)
                whole[rows, A] = (
                    get(part, own, A) + get(ra, 4 - 2 * x, rows) + get(ra, 3 + 2 * x, rows) + get(ra, 6, rows)
                )
                whole[rows, BL] = (
                    get(part, own, BL) + get(rbx, 0, rows, pl.ds(0, HALF)) + get(rbz, 4, rows) + get(rbz, 3, rows)
                )
                whole[rows, BR] = (
                    get(part, own, BR) + get(rbx, 0, rows, pl.ds(HALF, HALF)) + get(rbz, 2, rows) + get(rbz, 5, rows)
                )
            loop(BLOCK // 16, body)

        return first_a, first_b, s1, s1x, s2, s2x, s3, s4

    def turn(whole, held, stage):
        def body(n):
            cols = tile(n)
            v = whole[:, cols] * signs(cols)
            hi = v.astype(BF16)
            lo = (v - hi.astype(F32)).astype(BF16)
            y = dot(hi, had[...]) + dot(lo, had[...])
            stage[:, cols] = (held[:, cols].astype(F32) + y * UNIT).astype(BF16)
        loop(D // TILE, body, 4)

    def gather(out, stage, device, r):
        c = {}
        rx = lax.rem(r, 2)

        def go(zz, xx, cols, device):
            here = out.at[block(2 * zz + xx), cols]
            return push(here, here, device)

        def shift():
            c["s"] = push(stage, out.at[mine], device)

        def g1():
            c["s"].wait_recv()
            c["ax"] = go(z, rx, A, side)
            c["bm0"] = go(z, rx, B, up)
            c["bp0"] = go(z, rx, B, down)
            c["am0"] = go(z, rx, A, up)
            c["ap0"] = go(z, rx, A, down)
            c["bx0"] = go(z, rx, B, side)

        def g2():
            c["bm0"].wait_recv()
            c["bm1"] = go(zm, rx, BL, up)
            c["bx1"] = go(zm, rx, B, side)
            c["bp0"].wait_recv()
            c["bp1"] = go(zp, rx, BR, down)
            c["bx2"] = go(zp, rx, B, side)
            c["ax"].wait_recv()
            c["am1"] = go(z, 1 - rx, A, up)
            c["ap1"] = go(z, 1 - rx, A, down)
            c["am0"].wait_recv()
            c["am2"] = go(zm, rx, A, up)

        def g3():
            c["bm1"].wait_recv()
            c["bx3"] = go(z2, rx, BL, side)
            c["bp1"].wait_recv()
            c["bx4"] = go(z2, rx, BR, side)
            c["ap1"].wait_recv()
            c["ap2"] = go(zp, 1 - rx, A, down)

        def g4():
            for name in ("ap0", "am1", "am2", "ap2", "bx0", "bx1", "bx2", "bx3", "bx4"):
                c[name].wait_recv()

        return shift, g1, g2, g3, g4

    fa, fb, fs1, fs1x, fs2, fs2x, fs3, fs4 = scatter(fv, ra_f, rbx_f, rbz_f, total)
    ba, bb, bs1, bs1x, bs2, bs2x, bs3, bs4 = scatter(sv, ra_b, rbx_b, rbz_b, total)
    f_shift, fg1, fg2, fg3, fg4 = gather(of, stage_f, after, held_f)
    b_shift, bg1, bg2, bg3, bg4 = gather(ob, stage_b, before, held_b)

    rows_scale[...] = jnp.zeros_like(rows_scale)
    for one in l_fin:
        one.wait()

    def weighted_front(n):
        cols = tile(n)
        y = dot(fv[:, cols], had[...])
        fv[:, cols] = (y * (signs(cols) * gain[pl.ds(front, 1), cols] * UNIT)).astype(BF16)
        y = y * y
        rows_scale[...] += y[:, :128] + y[:, 128:]
    loop(D // TILE, weighted_front, 4)
    l_wo.start()
    scales(1.0 / HB)
    l_wk.wait()
    l_wv.wait()
    l_wq.wait()
    project(fv, front)
    for one in (l_sav, l_gin, l_fr, l_sr, l_gr):
        one.start()

    for h in range(HEADS):
        cols = pl.ds(h * HD, HD)
        for lo in (0, 256):
            rows = pl.ds(lo, 256)
            e, r = weights(qv[rows, cols], lo, 256)
            ctx[rows, cols] = (dot(e.astype(BF16), kvv[pl.ds(0, lo + 256), pl.ds(HD, HD)]) * r).astype(BF16)
    l_wo.wait()

    def project_out(n):
        cols = tile(n)
        fv[:, cols] = dot(ctx[...], wov[front, :, cols]).astype(BF16)
    loop(CA // TILE, project_out, 3)
    pl.semaphore_wait(barrier, 5)
    fa()
    loop(CB // TILE, project_out, 7, CA // TILE)
    fb()

    rows_scale[...] = jnp.zeros_like(rows_scale)
    l_sav.wait()
    l_gin.wait()

    def weighted_back(n):
        cols = tile(n)
        v = sv[:, cols].astype(F32)
        sv[:, cols] = (v * gain[pl.ds(back, 1), cols]).astype(BF16)
        v = v * v
        rows_scale[...] += v[:, :128] + v[:, 128:]
        gv[:, cols] = (dot(gv[:, cols], had[...]) * (signs(cols) * UNIT)).astype(BF16)
    loop(D // TILE, weighted_back, 4)
    scales(1.0)
    project(sv, back)
    fs1()
    fs1x()
    for n in range(2):
        rows = pl.ds(n * TILE, TILE)
        dctx[:, rows] = dot_nt(gv[...], wov[back, rows, :]).astype(BF16)
    fs2()
    dkv[...] = jnp.zeros_like(dkv)

    def attend_back(h):
        cols = pl.ds(h * HD, HD)
        for lo in (0, 256):
            rows, n = pl.ds(lo, 256), pl.ds(0, lo + 256)
            q, d = qv[rows, cols], dctx[rows, cols]
            e, r = weights(q, lo, 256)
            probs = e * r
            dkv[pl.ds(HD, HD), n] += dot_tn(d, probs.astype(BF16))
            dp = dot_nt(d, kvv[n, pl.ds(HD, HD)])
            ds = (probs * (dp - jnp.sum(probs * dp, axis=-1, keepdims=True))).astype(BF16)
            dq[rows, cols] = (dot(ds, kvv[n, pl.ds(0, HD)]) * SM).astype(BF16)
            dkv[pl.ds(0, HD), n] += dot_tn(q, ds)
    attend_back(0)
    attend_back(1)
    fs2x()
    attend_back(2)
    attend_back(3)
    dkvb[...] = dkv[...].astype(BF16)
    fs3()

    def pull_in(n):
        cols = tile(n)
        sv[:, cols] = (dot_nt(dq[...], wqv[back, cols, :]) + dot_nt(dkvb[...].T, wkv[back, cols, :])).astype(BF16)
    loop(CA // TILE, pull_in, 3)
    ba()
    loop(CB // TILE, pull_in, 7, CA // TILE)
    bb()

    fs4()
    l_fr.wait()
    turn(total, fr, stage_f)
    f_shift()
    bs1()
    bs1x()
    bs2()
    bs2x()
    bs3()
    fg1()
    bs4()
    l_sr.wait()
    l_gr.wait()

    def norm_back(i):
        rows = tile(i, 16)
        v = sr[rows, :].astype(F32)
        s = lax.rsqrt(jnp.sum(v * v, axis=-1, keepdims=True) * (1.0 / D) + EPS)
        g = total[rows, :] * gain[pl.ds(back, 1), :]
        inner = jnp.sum(v * g, axis=-1, keepdims=True)
        total[rows, :] = s * g - v * (s * s * s * inner * (1.0 / D))
    loop(BLOCK // 16, norm_back)
    turn(total, gr, stage_b)
    b_shift()
    fg2()
    fg3()
    bg1()
    fg4()
    bg2()
    bg3()
    bg4()
    for copy in started:
        copy.wait_send()


def local(forward_input, saved_input, gradient_input, roster, sign_bits, gain, w_query, w_key, w_value, w_out):
    vm = lambda shape, kind=BF16: pltpu.VMEM(shape, kind)
    anywhere = pl.BlockSpec(memory_space=pl.ANY)
    inside = pl.BlockSpec(memory_space=pltpu.VMEM)
    sums = [vm((7, BLOCK, CA)), vm((4, BLOCK, CB)), vm((6, BLOCK, HALF))]
    out = pltpu.VMEM((ROWS, D), BF16)
    arrived, returned = pl.pallas_call(
        kernel,
        out_shape=(out, out),
        in_specs=[pl.BlockSpec(memory_space=pltpu.SMEM), inside, inside] + [anywhere] * 7,
        out_specs=(inside, inside),
        scratch_shapes=[
            vm((ROWS, D)), vm((ROWS, D)), vm((ROWS, D)),
            vm((2, D, HEADS * HD)), vm((2, D, 2 * HD)), vm((2, HEADS * HD, D)),
            vm((BLOCK, D)), vm((BLOCK, D)), vm((BLOCK, D)),
            vm((2 * HB, 2 * HB)), vm((ROWS, 128), F32),
            vm((ROWS, HEADS * HD)), vm((ROWS, 2 * HD)), vm((ROWS, HEADS * HD)), vm((ROWS, HEADS * HD)),
            vm((ROWS, HEADS * HD)), vm((2 * HD, ROWS), F32), vm((2 * HD, ROWS)),
            *sums, *sums, vm((BLOCK, D), F32), vm((BLOCK, D)), vm((BLOCK, D)),
            pltpu.SemaphoreType.DMA((13,)), pltpu.SemaphoreType.DMA((68,)), pltpu.SemaphoreType.DMA((68,)),
        ],
        compiler_params=pltpu.CompilerParams(
            collective_id=0, has_side_effects=True, vmem_limit_bytes=51 * 2**20
        ),
        cost_estimate=pl.CostEstimate(flops=16 * 10**9, bytes_accessed=45 * 10**6, transcendentals=2 * 10**6),
        name="relay_slot",
    )(
        roster[0], sign_bits[None], gain[0], forward_input[0], saved_input[0], gradient_input[0],
        w_query[0], w_key[0], w_value[0], w_out[0],
    )
    return (arrived[None], returned[None])


def solution(mesh):
    placed = (
        P("pipe", None, None),
        P("pipe", None, None),
        P("pipe", None, None),
        P("pipe", None),
        P(),
        P("pipe", None, None),
        P("pipe", None, None, "tensor"),
        P("pipe", None, None, "tensor"),
        P("pipe", None, None, "tensor"),
        P("pipe", None, "tensor", None),
    )
    return jax.shard_map(
        local,
        mesh=mesh,
        in_specs=placed,
        out_specs=(P("pipe", None, None), P("pipe", None, None)),
        check_vma=False,
    )
```

```python
import functools
import math

import jax
import jax.numpy as jnp
from jax import lax
from jax.experimental import pallas as pl
from jax.experimental.pallas import tpu as pltpu
from jax.sharding import PartitionSpec as P

MESH = pl.DeviceIdType.MESH
D = 4096
ROWS = 512
HD = 128
HB = 128
HEADS = 4
BLOCK = 64
CA = 2304
CB = D - CA
HALF = CB // 2
TILE = 256
EPS = 1e-05
UNIT = 1.0 / math.sqrt(HB)
SM = 1.0 / math.sqrt(HD)
A = pl.ds(0, CA)
B = pl.ds(CA, CB)
BL = pl.ds(CA, HALF)
BR = pl.ds(CA + HALF, HALF)
F32 = jnp.float32
BF16 = jnp.bfloat16


def dot(a, b):
    return jnp.dot(a, b, preferred_element_type=F32)


def dot_nt(a, b):
    return lax.dot_general(a, b, (((1,), (1,)), ((), ())), preferred_element_type=F32)


def dot_tn(a, b):
    return lax.dot_general(a, b, (((0,), (0,)), ((), ())), preferred_element_type=F32)


def tile(c, width=TILE):
    return pl.ds(pl.multiple_of(c * width, width), width)


def loop(count, body, unroll=1, start=0):
    lax.fori_loop(start, start + count, lambda i, _: (body(i), 0)[1], 0, unroll=unroll)


def hadamard_pair():
    i = lax.broadcasted_iota(jnp.int32, (2 * HB, 2 * HB), 0)
    j = lax.broadcasted_iota(jnp.int32, (2 * HB, 2 * HB), 1)
    c = i & j & (HB - 1)
    c = c ^ (c >> 4)
    c = c ^ (c >> 2)
    c = c ^ (c >> 1)
    value = (1 - 2 * (c & 1)).astype(F32)
    return jnp.where((i >> 7) == (j >> 7), value, 0.0).astype(BF16)


def kernel(
    roster, bits, gain, fin, sav, gin, wq, wk, wv, wo,
    of, ob,
    fv, sv, gv, wqv, wkv, wov, fr, sr, gr,
    had, rows_scale, qv, kvv, ctx, dctx, dq, dkv, dkvb,
    ra_f, rbx_f, rbz_f, ra_b, rbx_b, rbz_b, total, stage_f, stage_b,
    load, send, recv,
):
    p = lax.axis_index("pipe")
    t = lax.axis_index("tensor")
    x = lax.rem(t, 2)
    z = lax.div(t, 2)
    n_pipe = lax.axis_size("pipe")
    zp, z2, zm = lax.rem(z + 1, 4), lax.rem(z + 2, 4), lax.rem(z + 3, 4)
    par = lax.rem(p, 2)
    swap = 1 - 2 * x
    up, down, side = (p, zp * 2 + x), (p, zm * 2 + x), (p, t + swap)
    after = (lax.rem(p + 1, n_pipe), t + par * swap)
    before = (lax.rem(p + n_pipe - 1, n_pipe), t + (1 - par) * swap)
    held_f = t + (1 - par) * swap
    held_b = t + par * swap

    def block(index):
        return pl.ds(pl.multiple_of(index * BLOCK, BLOCK), BLOCK)

    mine = block(t)
    loads = [
        (wk, wkv.at[:, :, pl.ds(0, HD)]), (wv, wkv.at[:, :, pl.ds(HD, HD)]), (wq, wqv), (wo, wov),
        (sav, sv), (gin, gv), (fin.at[mine], fr), (sav.at[mine], sr), (gin.at[mine], gr),
    ]
    quarters = [pl.ds(i * 128, 128) for i in range(4)]
    loads += [(fin.at[rows], fv.at[rows]) for rows in quarters]
    loads = [pltpu.make_async_copy(a, b, load.at[i]) for i, (a, b) in enumerate(loads)]
    l_wk, l_wv, l_wq, l_wo, l_sav, l_gin, l_fr, l_sr, l_gr, *l_fin = loads
    for one in (*l_fin, l_wk, l_wv, l_wq):
        one.start()

    barrier = pltpu.get_barrier_semaphore()
    for other in (up, down, side, after, before):
        pl.semaphore_signal(barrier, inc=1, device_id=other, device_id_type=MESH)

    front, back = roster[0], roster[1]
    had[...] = hadamard_pair()

    def signs(cols):
        return (2 * bits[:, cols] - 1).astype(F32)

    counter = [0]
    started = []

    def push(src, dst, device):
        i = counter[0]
        counter[0] += 1
        copy = pltpu.make_async_remote_copy(
            src_ref=src, dst_ref=dst, send_sem=send.at[i], recv_sem=recv.at[i], device_id=device, device_id_type=MESH
        )
        copy.start()
        started.append(copy)
        return copy

    def scales(factor):
        total_square = jnp.sum(rows_scale[...], axis=-1, keepdims=True)
        rows_scale[...] = jnp.broadcast_to(lax.rsqrt(total_square * (factor / D) + EPS), (ROWS, 128))

    def project(ref, which):
        s = rows_scale[...]
        s2 = jnp.concatenate([s, s], axis=1)
        kvv[...] = (dot(ref[...], wkv[which]) * s2).astype(BF16)
        for n in range(2):
            cols = pl.ds(n * TILE, TILE)
            qv[:, cols] = (dot(ref[...], wqv[which, :, cols]) * (s2 * SM)).astype(BF16)

    def weights(q, lo, size):
        n = lo + size
        s = dot_nt(q, kvv[pl.ds(0, n), pl.ds(0, HD)])
        row = lax.broadcasted_iota(jnp.int32, (size, n), 0) + lo
        col = lax.broadcasted_iota(jnp.int32, (size, n), 1)
        s = jnp.where(row >= col, s, -1e30)
        e = jnp.exp(s - jnp.max(s, axis=-1, keepdims=True))
        return e, 1.0 / jnp.sum(e, axis=-1, keepdims=True)

    def add(ref, base, cols, *terms):
        def body(i):
            rows = pl.ds(pl.multiple_of(base * BLOCK + i * 16, 16), 16)
            value = ref[rows, cols].astype(F32)
            for term in terms:
                value += term[pl.ds(pl.multiple_of(i * 16, 16), 16), :].astype(F32)
            ref[rows, cols] = value.astype(BF16)
        loop(BLOCK // 16, body)

    def scatter(part, ra, rbx, rbz, whole):
        c = {}

        def first_a():
            c["m0"] = push(part.at[block(2 * z2), A], ra.at[0], up)
            c["p0"] = push(part.at[block(2 * z2 + 1), A], ra.at[1], down)
            c["m1"] = push(part.at[block(2 * zp + 1), A], ra.at[2], up)
            c["p1"] = push(part.at[block(2 * zm), A], ra.at[3], down)

        def first_b():
            for k, zz in ((2, z2), (1, zp), (3, zm), (0, z)):
                c["x", k] = push(part.at[block(2 * zz + 1 - x), B], rbx.at[k], side)

        def s1():
            c["m0"].wait_recv()
            add(part, 2 * zp, A, ra.at[0])
            c["m2"] = push(part.at[block(2 * zp), A], ra.at[4], up)
            c["p0"].wait_recv()
            add(part, 2 * zm + 1, A, ra.at[1])
            c["p2"] = push(part.at[block(2 * zm + 1), A], ra.at[5], down)

        def s1x():
            c["x", 2].wait_recv()
            add(part, 2 * z2 + x, B, rbx.at[2])
            c["bm0"] = push(part.at[block(2 * z2 + x), BL], rbz.at[0], up)
            c["bp0"] = push(part.at[block(2 * z2 + x), BR], rbz.at[1], down)

        def s2():
            c["x", 1].wait_recv()
            add(part, 2 * zp + x, B, rbx.at[1])
            c["bm1"] = push(part.at[block(2 * zp + x), BR], rbz.at[2], up)

        def s2x():
            c["x", 3].wait_recv()
            add(part, 2 * zm + x, B, rbx.at[3])
            c["bp1"] = push(part.at[block(2 * zm + x), BL], rbz.at[3], down)

        def s2z():
            c["bm0"].wait_recv()
            add(part, 2 * zp + x, BL, rbz.at[0])
            c["bm2"] = push(part.at[block(2 * zp + x), BL], rbz.at[4], up)
            c["bp0"].wait_recv()
            add(part, 2 * zm + x, BR, rbz.at[1])
            c["bp2"] = push(part.at[block(2 * zm + x), BR], rbz.at[5], down)

        def s3():
            for name in ("m1", "m2", "p1", "p2"):
                c[name].wait_recv()
            add(part, 2 * z + 1 - x, A, ra.at[2 + 2 * x], ra.at[5 - 2 * x])
            c["ax"] = push(part.at[block(2 * z + 1 - x), A], ra.at[6], side)

        def s4():
            for name in ("ax", ("x", 0), "bm1", "bm2", "bp1", "bp2"):
                c[name].wait_recv()

            def body(i):
                rows = tile(i, 16)
                own = pl.ds(pl.multiple_of(t * BLOCK + i * 16, 16), 16)
                get = lambda ref, *at: ref[at].astype(F32)
                whole[rows, A] = (
                    get(part, own, A) + get(ra, 4 - 2 * x, rows) + get(ra, 3 + 2 * x, rows) + get(ra, 6, rows)
                )
                whole[rows, BL] = (
                    get(part, own, BL) + get(rbx, 0, rows, pl.ds(0, HALF)) + get(rbz, 4, rows) + get(rbz, 3, rows)
                )
                whole[rows, BR] = (
                    get(part, own, BR) + get(rbx, 0, rows, pl.ds(HALF, HALF)) + get(rbz, 2, rows) + get(rbz, 5, rows)
                )
            loop(BLOCK // 16, body)

        return first_a, first_b, s1, s1x, s2, s2x, s2z, s3, s4

    def turn(whole, held, stage):
        def body(n):
            cols = tile(n)
            v = whole[:, cols] * signs(cols)
            hi = v.astype(BF16)
            lo = (v - hi.astype(F32)).astype(BF16)
            y = dot(hi, had[...]) + dot(lo, had[...])
            stage[:, cols] = (held[:, cols].astype(F32) + y * UNIT).astype(BF16)
        loop(D // TILE, body, 4)

    def gather(out, stage, device, r):
        c = {}
        rx = lax.rem(r, 2)

        def go(zz, xx, cols, device):
            here = out.at[block(2 * zz + xx), cols]
            return push(here, here, device)

        def shift():
            c["s"] = push(stage, out.at[mine], device)

        def g1():
            c["s"].wait_recv()
            c["ax"] = go(z, rx, A, side)
            c["bm0"] = go(z, rx, B, up)
            c["bp0"] = go(z, rx, B, down)
            c["am0"] = go(z, rx, A, up)
            c["ap0"] = go(z, rx, A, down)
            c["bx0"] = go(z, rx, B, side)

        def g2():
            c["bm0"].wait_recv()
            c["bm1"] = go(zm, rx, BL, up)
            c["bx1"] = go(zm, rx, B, side)
            c["bp0"].wait_recv()
            c["bp1"] = go(zp, rx, BR, down)
            c["bx2"] = go(zp, rx, B, side)
            c["ax"].wait_recv()
            c["am1"] = go(z, 1 - rx, A, up)
            c["ap1"] = go(z, 1 - rx, A, down)
            c["am0"].wait_recv()
            c["am2"] = go(zm, rx, A, up)

        def g3():
            c["bm1"].wait_recv()
            c["bx3"] = go(z2, rx, BL, side)
            c["bp1"].wait_recv()
            c["bx4"] = go(z2, rx, BR, side)
            c["ap1"].wait_recv()
            c["ap2"] = go(zp, 1 - rx, A, down)

        def g4():
            for name in ("ap0", "am1", "am2", "ap2", "bx0", "bx1", "bx2", "bx3", "bx4"):
                c[name].wait_recv()

        return shift, g1, g2, g3, g4

    fa, fb, fs1, fs1x, fs2, fs2x, fs2z, fs3, fs4 = scatter(fv, ra_f, rbx_f, rbz_f, total)
    ba, bb, bs1, bs1x, bs2, bs2x, bs2z, bs3, bs4 = scatter(sv, ra_b, rbx_b, rbz_b, total)
    f_shift, fg1, fg2, fg3, fg4 = gather(of, stage_f, after, held_f)
    b_shift, bg1, bg2, bg3, bg4 = gather(ob, stage_b, before, held_b)

    rows_scale[...] = jnp.zeros_like(rows_scale)
    for one in l_fin:
        one.wait()

    def weighted_front(n):
        cols = tile(n)
        y = dot(fv[:, cols], had[...])
        fv[:, cols] = (y * (signs(cols) * gain[pl.ds(front, 1), cols] * UNIT)).astype(BF16)
        y = y * y
        rows_scale[...] += y[:, :128] + y[:, 128:]
    loop(D // TILE, weighted_front, 4)
    l_wo.start()
    scales(1.0 / HB)
    l_wk.wait()
    l_wv.wait()
    l_wq.wait()
    project(fv, front)
    for one in (l_sav, l_gin, l_fr, l_sr, l_gr):
        one.start()

    for h in range(HEADS):
        cols = pl.ds(h * HD, HD)
        for lo in (0, 256):
            rows = pl.ds(lo, 256)
            e, r = weights(qv[rows, cols], lo, 256)
            ctx[rows, cols] = (dot(e.astype(BF16), kvv[pl.ds(0, lo + 256), pl.ds(HD, HD)]) * r).astype(BF16)
    l_wo.wait()

    def project_out(n):
        cols = tile(n)
        fv[:, cols] = dot(ctx[...], wov[front, :, cols]).astype(BF16)
    loop(CA // TILE, project_out, 3)
    pl.semaphore_wait(barrier, 5)
    fa()
    loop(CB // TILE, project_out, 7, CA // TILE)
    fb()

    rows_scale[...] = jnp.zeros_like(rows_scale)
    l_sav.wait()
    l_gin.wait()

    def weighted_back(n):
        cols = tile(n)
        v = sv[:, cols].astype(F32)
        sv[:, cols] = (v * gain[pl.ds(back, 1), cols]).astype(BF16)
        v = v * v
        rows_scale[...] += v[:, :128] + v[:, 128:]
        gv[:, cols] = (dot(gv[:, cols], had[...]) * (signs(cols) * UNIT)).astype(BF16)
    loop(D // TILE, weighted_back, 4)
    scales(1.0)
    fs1()
    fs1x()
    project(sv, back)
    for n in range(2):
        rows = pl.ds(n * TILE, TILE)
        dctx[:, rows] = dot_nt(gv[...], wov[back, rows, :]).astype(BF16)
    fs2()
    dkv[...] = jnp.zeros_like(dkv)

    def attend_back(h):
        cols = pl.ds(h * HD, HD)
        for lo in (0, 256):
            rows, n = pl.ds(lo, 256), pl.ds(0, lo + 256)
            q, d = qv[rows, cols], dctx[rows, cols]
            e, r = weights(q, lo, 256)
            probs = e * r
            dkv[pl.ds(HD, HD), n] += dot_tn(d, probs.astype(BF16))
            dp = dot_nt(d, kvv[n, pl.ds(HD, HD)])
            ds = (probs * (dp - jnp.sum(probs * dp, axis=-1, keepdims=True))).astype(BF16)
            dq[rows, cols] = (dot(ds, kvv[n, pl.ds(0, HD)]) * SM).astype(BF16)
            dkv[pl.ds(0, HD), n] += dot_tn(q, ds)
    attend_back(0)
    attend_back(1)
    fs2x()
    attend_back(2)
    attend_back(3)
    dkvb[...] = dkv[...].astype(BF16)
    fs2z()
    fs3()

    def pull_in(n):
        cols = tile(n)
        sv[:, cols] = (dot_nt(dq[...], wqv[back, cols, :]) + dot_nt(dkvb[...].T, wkv[back, cols, :])).astype(BF16)
    loop(CA // TILE, pull_in, 3)
    ba()
    loop(CB // TILE, pull_in, 7, CA // TILE)
    bb()

    fs4()
    l_fr.wait()
    turn(total, fr, stage_f)
    f_shift()
    bs1()
    bs1x()
    bs2()
    bs2x()
    bs2z()
    bs3()
    fg1()
    bs4()
    l_sr.wait()
    l_gr.wait()

    def norm_back(i):
        rows = tile(i, 16)
        v = sr[rows, :].astype(F32)
        s = lax.rsqrt(jnp.sum(v * v, axis=-1, keepdims=True) * (1.0 / D) + EPS)
        g = total[rows, :] * gain[pl.ds(back, 1), :]
        inner = jnp.sum(v * g, axis=-1, keepdims=True)
        total[rows, :] = s * g - v * (s * s * s * inner * (1.0 / D))
    loop(BLOCK // 16, norm_back)
    turn(total, gr, stage_b)
    b_shift()
    fg2()
    fg3()
    bg1()
    fg4()
    bg2()
    bg3()
    bg4()
    for copy in started:
        copy.wait_send()


def local(forward_input, saved_input, gradient_input, roster, sign_bits, gain, w_query, w_key, w_value, w_out):
    vm = lambda shape, kind=BF16: pltpu.VMEM(shape, kind)
    anywhere = pl.BlockSpec(memory_space=pl.ANY)
    inside = pl.BlockSpec(memory_space=pltpu.VMEM)
    sums = [vm((7, BLOCK, CA)), vm((4, BLOCK, CB)), vm((6, BLOCK, HALF))]
    out = pltpu.VMEM((ROWS, D), BF16)
    arrived, returned = pl.pallas_call(
        kernel,
        out_shape=(out, out),
        in_specs=[pl.BlockSpec(memory_space=pltpu.SMEM), inside, inside] + [anywhere] * 7,
        out_specs=(inside, inside),
        scratch_shapes=[
            vm((ROWS, D)), vm((ROWS, D)), vm((ROWS, D)),
            vm((2, D, HEADS * HD)), vm((2, D, 2 * HD)), vm((2, HEADS * HD, D)),
            vm((BLOCK, D)), vm((BLOCK, D)), vm((BLOCK, D)),
            vm((2 * HB, 2 * HB)), vm((ROWS, 128), F32),
            vm((ROWS, HEADS * HD)), vm((ROWS, 2 * HD)), vm((ROWS, HEADS * HD)), vm((ROWS, HEADS * HD)),
            vm((ROWS, HEADS * HD)), vm((2 * HD, ROWS), F32), vm((2 * HD, ROWS)),
            *sums, *sums, vm((BLOCK, D), F32), vm((BLOCK, D)), vm((BLOCK, D)),
            pltpu.SemaphoreType.DMA((13,)), pltpu.SemaphoreType.DMA((68,)), pltpu.SemaphoreType.DMA((68,)),
        ],
        compiler_params=pltpu.CompilerParams(
            collective_id=0, has_side_effects=True, vmem_limit_bytes=51 * 2**20
        ),
        cost_estimate=pl.CostEstimate(flops=16 * 10**9, bytes_accessed=45 * 10**6, transcendentals=2 * 10**6),
        name="relay_slot",
    )(
        roster[0], sign_bits[None], gain[0], forward_input[0], saved_input[0], gradient_input[0],
        w_query[0], w_key[0], w_value[0], w_out[0],
    )
    return (arrived[None], returned[None])


def solution(mesh):
    placed = (
        P("pipe", None, None),
        P("pipe", None, None),
        P("pipe", None, None),
        P("pipe", None),
        P(),
        P("pipe", None, None),
        P("pipe", None, None, "tensor"),
        P("pipe", None, None, "tensor"),
        P("pipe", None, None, "tensor"),
        P("pipe", None, "tensor", None),
    )
    return jax.shard_map(
        local,
        mesh=mesh,
        in_specs=placed,
        out_specs=(P("pipe", None, None), P("pipe", None, None)),
        check_vma=False,
    )
```
